128 devices in a mesh: gx: 16 (over y, x), gy: 8 (over z, core).
Axes of the slice: x: 4, y: 4, z: 4, core: 2. Of those that a mesh axis runs over, the one named last changes fastest.
Arguments:
- initial_state: float32 [16384, 16384], P(('gx', 'gy')), may hold values from -16 to 16
- edge_list: int32 [56, 2], replicated, may hold values from 0 to 27, as said below
- couplings: float32 [56], replicated, may hold values from -0.15 to 0.15
- gates_low: float32 [6, 128, 128], replicated, may hold values from -2 to 2
- gates_mid: float32 [6, 128, 128], replicated, may hold values from -2 to 2
- gates_high: float32 [6, 128, 128], replicated, may hold values from -2 to 2
- top_gate: float32 [128, 128], replicated, may hold values from -2 to 2
Outputs:
- evolved: float32 [16384, 16384], P(('gx', 'gy'))
The draws below stay inside these ranges and needn't reach their ends.
Inputs may be any that keep to these rules, and one draw needn't show every extreme that they name: `edge_list`: each row names two different spins; every spin is named by some row.
All inputs are finite; a program needn't handle non-finite values.
Results may differ from the reference program's by a relative error of at most 0.0003.
Values sent between devices are 32-bit elements; how exact they have to be, the bound alone decides.
No kernel may reach another device: no remote copies, remote signals or barrier semaphores. Data moves between devices by JAX's collectives and lax.ppermute only.
A program may use at most 128 MiB of HBM per device.

```python
import jax
import jax.numpy as jnp
from jax import lax

HIGH_BITS = 7
BLOCK_BITS = 7
LAYERS = 6
HIGH = 128
BLOCK = 128
GLOBAL_BITS = 7
QUBITS = 28
EDGES = 56
ROWS = 16384
N_GX = 16
N_GY = 8


def near_identity(diag_key, offdiag, count, size_value):
    diagonal = jax.random.uniform(diag_key, (count, size_value, 1), jnp.float32, 0.8, 1.2)
    identity = (jnp.arange(size_value)[:, None] == jnp.arange(size_value)[None, :]).astype(jnp.float32)
    return diagonal * identity[None] + offdiag * (0.35 / jnp.sqrt(jnp.float32(size_value)))


def draw_initial_state(key, part):
    key = jax.random.fold_in(key, 1)
    first_key = jax.random.fold_in(key, 0)
    shape = (ROWS, BLOCK * BLOCK)
    position = jnp.arange(ROWS, dtype=jnp.float32)[:, None] / ROWS
    ramp_scale = 1.0 + 1.5 * position
    base_values = jnp.clip(jax.random.normal(first_key, shape, jnp.float32), -6.0, 6.0)
    values = base_values * ramp_scale
    return values.astype(jnp.float32)


def draw_edge_list(key, part):
    key = jax.random.fold_in(key, 2)
    first_key, second_key, third_key = jax.random.split(key, 3)
    starts = jnp.concatenate([jax.random.permutation(first_key, QUBITS).astype(jnp.int32), jax.random.randint(second_key, (EDGES - QUBITS,), 0, QUBITS, jnp.int32)])
    offsets = jax.random.randint(third_key, (EDGES,), 1, QUBITS, jnp.int32)
    second = (starts + offsets) % QUBITS
    return jnp.stack([starts, second], axis=1).astype(jnp.int32)


def draw_gates_low(key, part):
    key = jax.random.fold_in(key, 3)
    first_key, second_key = jax.random.split(key)
    shape = (LAYERS, BLOCK, BLOCK)
    offdiag = jnp.clip(jax.random.normal(second_key, shape, jnp.float32), -4.0, 4.0)
    return near_identity(first_key, offdiag, LAYERS, BLOCK).astype(jnp.float32)


def draw_gates_mid(key, part):
    key = jax.random.fold_in(key, 4)
    first_key, second_key = jax.random.split(key)
    shape = (LAYERS, BLOCK, BLOCK)
    offdiag = jnp.clip(jax.random.normal(second_key, shape, jnp.float32), -4.0, 4.0)
    return near_identity(first_key, offdiag, LAYERS, BLOCK).astype(jnp.float32)


def draw_gates_high(key, part):
    key = jax.random.fold_in(key, 5)
    first_key, second_key = jax.random.split(key)
    shape = (LAYERS, HIGH, HIGH)
    offdiag = jnp.clip(jax.random.normal(second_key, shape, jnp.float32), -4.0, 4.0)
    return near_identity(first_key, offdiag, LAYERS, HIGH).astype(jnp.float32)


def draw_top_gate(key, part):
    key = jax.random.fold_in(key, 6)
    first_key, second_key = jax.random.split(key)
    shape = (1, HIGH, HIGH)
    offdiag = jnp.clip(jax.random.normal(second_key, shape, jnp.float32), -4.0, 4.0)
    return near_identity(first_key, offdiag, 1, HIGH)[0].astype(jnp.float32)


def scatter_about(stream_key, shape, width, most, kind=jnp.bfloat16):
    drawn = width * jax.random.normal(stream_key, shape, jnp.float32)
    return jnp.clip(drawn, min=-most, max=most).astype(kind)


def setup_inputs(seed: int = 0) -> dict:
    seeds = jax.random.split(jax.random.key(seed), 8)
    initial_state = draw_initial_state(jax.random.fold_in(seeds[7], 71), 0)
    edge_list = draw_edge_list(jax.random.fold_in(seeds[7], 71), 0)
    couplings = scatter_about(seeds[2], (EDGES,), 0.03, 0.15, jnp.float32)
    gates_low = draw_gates_low(jax.random.fold_in(seeds[7], 71), 0)
    gates_mid = draw_gates_mid(jax.random.fold_in(seeds[7], 71), 0)
    gates_high = draw_gates_high(jax.random.fold_in(seeds[7], 71), 0)
    top_gate = draw_top_gate(jax.random.fold_in(seeds[7], 71), 0)
    return {"initial_state": initial_state, "edge_list": edge_list, "couplings": couplings, "gates_low": gates_low, "gates_mid": gates_mid, "gates_high": gates_high, "top_gate": top_gate}


highest = lax.Precision.HIGHEST

def spin_signs(index_list, bit_count):
    shift_amounts = bit_count - 1 - jnp.arange(bit_count, dtype=jnp.int32)
    bit_values = jnp.right_shift(index_list[:, None], shift_amounts[None, :]) & 1
    return (1 - 2 * bit_values).astype(jnp.float32)

def coupling_matrix(edge_list, couplings, qubit_count):
    qubit_names = jnp.arange(qubit_count, dtype=jnp.int32)
    first_end = (edge_list[:, 0:1] == qubit_names[None, :]).astype(jnp.float32)
    second_end = (edge_list[:, 1:2] == qubit_names[None, :]).astype(jnp.float32)
    return jnp.dot((first_end * couplings[:, None]).T, second_end, precision=highest)

def energy_field(row_ids, row_bits, col_ids, col_bits, matrix):
    row_spins = spin_signs(row_ids, row_bits)
    col_spins = spin_signs(col_ids, col_bits)
    row_block = matrix[:row_bits, :row_bits]
    col_block = matrix[row_bits:, row_bits:]
    mixed_block = matrix[:row_bits, row_bits:] + matrix[row_bits:, :row_bits].T
    row_energy = lax.optimization_barrier(jnp.sum(jnp.dot(row_spins, row_block, precision=highest) * row_spins, axis=1))
    col_energy = lax.optimization_barrier(jnp.sum(jnp.dot(col_spins, col_block, precision=highest) * col_spins, axis=1))
    cross_term = jnp.dot(jnp.dot(row_spins, mixed_block, precision=highest), col_spins.T, precision=highest)
    return row_energy[:, None] + col_energy[None, :] + cross_term

def reference(initial_state, edge_list, couplings, gates_low, gates_mid, gates_high, top_gate):
    devices = N_GX * N_GY
    plane_size = BLOCK * BLOCK
    row_bits = GLOBAL_BITS + HIGH_BITS
    matrix = coupling_matrix(edge_list, couplings, QUBITS)
    factor = jnp.exp(energy_field(jnp.arange(ROWS, dtype=jnp.int32), row_bits, jnp.arange(plane_size, dtype=jnp.int32), 2 * BLOCK_BITS, matrix))
    amplitudes = initial_state
    for layer_index in range(LAYERS):
        amplitudes = (amplitudes * factor).reshape(ROWS, BLOCK, BLOCK)
        amplitudes = jnp.einsum('rml,kl->rmk', amplitudes, gates_low[layer_index], precision=highest)
        amplitudes = jnp.einsum('rml,km->rkl', amplitudes, gates_mid[layer_index], precision=highest)
        grouped = amplitudes.reshape(devices, HIGH, plane_size)
        grouped = jnp.einsum('ghc,kh->gkc', grouped, gates_high[layer_index], precision=highest)
        amplitudes = grouped.reshape(ROWS, plane_size)
    sliver = HIGH // devices
    grouped = amplitudes.reshape(devices, devices, sliver, plane_size).transpose(1, 0, 2, 3)
    grouped = grouped.reshape(devices, HIGH, plane_size)
    grouped = jnp.einsum('ij,pjc->pic', top_gate, grouped, precision=highest)
    rotated = grouped.reshape(devices, devices, sliver, plane_size).transpose(1, 0, 2, 3)
    rotated = rotated.reshape(ROWS, plane_size)
    final = rotated * factor
    mean_square = jnp.sum(final * final) / jnp.float32(ROWS * plane_size)
    return final / jnp.sqrt(mean_square + 1e-06)
```

```python
import jax
import jax.numpy as jnp
from jax import lax
from jax.experimental import pallas as pl
from jax.experimental.pallas import tpu as pltpu
from jax.sharding import PartitionSpec as P

HIGHEST = lax.Precision.HIGHEST
F32 = jnp.float32
BF16 = jnp.bfloat16
N = 128
BITS = 7
LAYERS = 6
AXES = ("gx", "gy")
GROUP = 32
PITCH = N + 8
MIX_GROUP = 16
PIECE = 8
VMEM_BYTES = 62 * 2**20


def mm(a, b):
    return lax.dot_general(a, b, (((1,), (0,)), ((), ())), preferred_element_type=F32)


def mm_exact(a, b):
    return jnp.dot(a, b, precision=HIGHEST, preferred_element_type=F32)


def mm_nt_exact(a, b):
    return lax.dot_general(
        a, b, (((1,), (1,)), ((), ())), precision=HIGHEST, preferred_element_type=F32
    )


def iota(axis):
    return lax.broadcasted_iota(jnp.int32, (N, N), axis)


def split(x):
    high = x.astype(BF16)
    low = (x - high.astype(F32)).astype(BF16)
    return high, low


def left_pack(gate):
    high, low = split(gate)
    return jnp.concatenate(
        [jnp.concatenate([high, high], axis=1), jnp.concatenate([low, low], axis=1)], axis=0
    )


def right_pack(gate):
    high, low = split(gate.T)
    row = jnp.concatenate([high, low], axis=1)
    return jnp.concatenate([row, row], axis=0)


def left_gate(pack, tiles):
    out = []
    for i in range(0, len(tiles), 2):
        high, low = split(jnp.concatenate(tiles[i : i + 2], axis=1))
        both = mm(pack, jnp.concatenate([high, low], axis=0))
        both = both[:N] + both[N:]
        out += [both[:, :N], both[:, N:]]
    return out


def right_gate(pack, tiles):
    out = []
    for i in range(0, len(tiles), 2):
        high, low = split(jnp.concatenate(tiles[i : i + 2], axis=0))
        both = mm(jnp.concatenate([high, low], axis=1), pack)
        both = both[:, :N] + both[:, N:]
        out += [both[:N], both[N:]]
    return out


def spins(start, value):
    qubit = iota(1)
    inside = (qubit >= start) & (qubit < start + BITS)
    shift = jnp.clip(start + BITS - 1 - qubit, 0, BITS - 1)
    bit = jnp.right_shift(value, shift) & 1
    return jnp.where(inside, 1 - 2 * bit, 0).astype(F32)


def coupling_matrix(edge_ref, coupling_ref):
    names = lax.broadcasted_iota(jnp.int32, (N, edge_ref.shape[1]), 0)
    first = (edge_ref[0:1, :] == names).astype(F32) * coupling_ref[...]
    second = (edge_ref[1:2, :] == names).astype(F32)
    one_way = mm_nt_exact(first, second)
    return one_way + one_way.T


def flat_position():
    return lax.axis_index("gx") * lax.axis_size("gy") + lax.axis_index("gy")


def pair_factors(matrix, fixed, rows, planes, lanes):
    row_field = mm_exact(rows, matrix)
    plane_field = mm_exact(planes, matrix)
    row_fixed = rows + fixed
    row_energy = jnp.sum(0.5 * mm_exact(row_fixed, matrix) * row_fixed, axis=1, keepdims=True)
    plane_energy = jnp.sum(plane_field * (0.5 * planes + fixed), axis=1, keepdims=True)
    lane_terms = mm_exact(lanes, matrix) * (0.5 * lanes + fixed)
    lane_energy = mm_nt_exact(jnp.ones((N, N), F32), lane_terms)
    over_lanes = jnp.exp(mm_nt_exact(row_field, lanes) + row_energy)
    over_rows = jnp.exp(mm_nt_exact(row_field, planes))
    over_planes = jnp.exp(mm_nt_exact(plane_field, lanes) + plane_energy + lane_energy)
    return over_lanes, over_rows, over_planes


def plane_tile(plane):
    return pl.ds(pl.multiple_of(plane * PITCH, 8), N)


def row_tile(row):
    return pl.ds(row, N, stride=PITCH)


def each(count, body):
    def step(i, c):
        body(i)
        return c

    lax.fori_loop(0, count, step, 0)


def sweep(body):
    each(N // GROUP, lambda i: body(i * GROUP))


def start_copies(sem, *pairs):
    copies = [pltpu.make_async_copy(source, target, sem.at[i]) for i, (source, target) in enumerate(pairs)]
    for copy in copies:
        copy.start()
    return copies


def evolve_kernel(edge_hbm, coupling_hbm, low_hbm, mid_hbm, high_hbm, state_ref, out_ref,
                  by_plane, by_row, factor, edge_ref, coupling_ref, low_ref, mid_ref, high_ref,
                  lane_part, plane_part, turning, packs, small_sem, in_sem, out_sem):
    def load(plane):
        columns = pl.ds(pl.multiple_of(plane * N, N), N)
        return pltpu.make_async_copy(state_ref.at[:, columns], by_plane.at[plane_tile(plane)], in_sem.at[plane])

    def store(plane):
        return pltpu.make_async_copy(by_plane.at[plane_tile(plane)], out_ref.at[plane], out_sem.at[plane])

    small = start_copies(
        small_sem,
        (edge_hbm, edge_ref), (coupling_hbm, coupling_ref),
        (high_hbm, high_ref), (low_hbm, low_ref), (mid_hbm, mid_ref),
    )
    each(N, lambda plane: load(plane).start())
    for copy in small[:2]:
        copy.wait()
    matrix = coupling_matrix(edge_ref, coupling_ref)
    lane_part[...], turning[...], plane_part[...] = pair_factors(
        matrix,
        spins(0, flat_position()),
        spins(BITS, iota(0)),
        spins(2 * BITS, iota(0)),
        spins(3 * BITS, iota(0)),
    )
    for copy in small[2:]:
        copy.wait()
    packs[0] = left_pack(high_ref[0])
    packs[1] = right_pack(low_ref[0])

    def first(plane):
        each(GROUP, lambda j: load(plane + j).wait())
        columns = turning[...]
        tiles = []
        for j in range(GROUP):
            scale = lane_part[...] * (plane_part[pl.ds(plane + j, 1), :] * columns[:, j : j + 1])
            factor[plane_tile(plane + j)] = scale
            tiles.append(by_plane[plane_tile(plane + j)] * scale)
        turning[...] = pltpu.roll(columns, N - GROUP, 1)
        tiles = right_gate(packs[1], left_gate(packs[0], tiles))
        for j in range(GROUP):
            by_plane[plane_tile(plane + j)] = tiles[j]

    sweep(first)

    for layer in range(1, LAYERS):
        rows_now = layer % 2 == 1
        across = mid_ref if rows_now else high_ref
        packs[0] = left_pack(across[layer - 1])
        packs[1] = left_pack(across[layer])
        packs[2] = right_pack(low_ref[layer])
        source, target = (by_plane, by_row) if rows_now else (by_row, by_plane)
        factor_tile = row_tile if rows_now else plane_tile

        def middle(index, source=source, target=target, factor_tile=factor_tile):
            tiles = [source[row_tile(index + j)] for j in range(GROUP)]
            tiles = left_gate(packs[0], tiles)
            tiles = [t * factor[factor_tile(index + j)] for j, t in enumerate(tiles)]
            tiles = right_gate(packs[2], left_gate(packs[1], tiles))
            for j in range(GROUP):
                target[plane_tile(index + j)] = tiles[j]

        sweep(middle)

    packs[0] = left_pack(high_ref[LAYERS - 1])

    def last(plane):
        tiles = left_gate(packs[0], [by_row[row_tile(plane + j)] for j in range(GROUP)])
        for j in range(GROUP):
            by_plane[plane_tile(plane + j)] = tiles[j]
        each(GROUP, lambda j: store(plane + j).start())

    sweep(last)
    each(N, lambda plane: store(plane).wait())


def mix_kernel(edge_hbm, coupling_hbm, top_hbm, in_ref, out_ref,
               tiles_in, tiles_out, squares, edge_ref, coupling_ref, top_ref, lane_part, plane_part, turning, pack,
               small_sem, in_sem, out_sem, squares_sem):
    def load(row):
        return pltpu.make_async_copy(in_ref.at[:, row], tiles_in.at[row], in_sem.at[row])

    def store(row):
        return pltpu.make_async_copy(tiles_out.at[row], out_ref.at[:, row], out_sem.at[row])

    small = start_copies(small_sem, (edge_hbm, edge_ref), (coupling_hbm, coupling_ref), (top_hbm, top_ref))
    each(N, lambda row: load(row).start())
    for copy in small:
        copy.wait()
    matrix = coupling_matrix(edge_ref, coupling_ref)
    lane_part[...], turning[...], plane_part[...] = pair_factors(
        matrix,
        spins(2 * BITS, flat_position()),
        spins(0, iota(0)),
        spins(BITS, iota(0)),
        spins(3 * BITS, iota(0)),
    )
    pack[...] = left_pack(top_ref[...])

    def turn(i, total):
        row = i * MIX_GROUP
        each(MIX_GROUP, lambda j: load(row + j).wait())
        columns = turning[...]
        tiles = left_gate(pack[...], [tiles_in[row + j] for j in range(MIX_GROUP)])
        for j in range(MIX_GROUP):
            scale = lane_part[...] * (plane_part[pl.ds(row + j, 1), :] * columns[:, j : j + 1])
            done = tiles[j] * scale
            tiles_out[row + j] = done
            total += jnp.sum((done * done).reshape(N // 8, 8, N), axis=0)
        turning[...] = pltpu.roll(columns, N - MIX_GROUP, 1)
        each(MIX_GROUP, lambda j: store(row + j).start())
        return total

    total = lax.fori_loop(0, N // MIX_GROUP, turn, jnp.zeros((8, N), F32))
    squares[...] = jnp.broadcast_to(total[None], squares.shape)
    last = pltpu.make_async_copy(squares, out_ref.at[:, pl.ds(N, 8)], squares_sem)
    last.start()
    each(N, lambda row: store(row).wait())
    last.wait()


def finish_kernel(in_ref, out_ref, held, squares, squares_sem, in_sem, out_sem):
    def load(piece):
        part = pl.ds(piece * PIECE, PIECE)
        return pltpu.make_async_copy(in_ref.at[part, pl.ds(0, N)], held.at[part], in_sem.at[piece])

    def store(plane):
        columns = pl.ds(pl.multiple_of(plane * N, N), N)
        return pltpu.make_async_copy(held.at[plane], out_ref.at[:, columns], out_sem.at[plane])

    squares_load = pltpu.make_async_copy(in_ref.at[:, pl.ds(N, 8)], squares, squares_sem)
    squares_load.start()
    each(N // PIECE, lambda piece: load(piece).start())
    squares_load.wait()
    total = jnp.sum(jnp.sum(squares[...], axis=0))
    mean_square = total / jnp.float32(N * N * N * N)
    scale = lax.rsqrt(jnp.full((8, N), mean_square + 1e-06, F32))

    def piece_step(piece):
        load(piece).wait()
        for j in range(PIECE):
            plane = piece * PIECE + j
            held[plane] = held[plane] * scale[0:1]
            store(plane).start()

    each(N // PIECE, piece_step)
    each(N, lambda plane: store(plane).wait())


def local(initial_state, edge_list, couplings, gates_low, gates_mid, gates_high, top_gate):
    edges = edge_list.T
    couplings = couplings.reshape(1, -1)
    hbm = pl.BlockSpec(memory_space=pltpu.HBM)
    square = pltpu.VMEM((N, N), F32)
    cube = pltpu.VMEM((N, N, N), F32)
    pitched = pltpu.VMEM((N * PITCH, N), F32)
    gates = pltpu.VMEM((LAYERS, N, N), F32)
    small = [pltpu.VMEM(edges.shape, jnp.int32), pltpu.VMEM(couplings.shape, F32)]
    sems = lambda count: pltpu.SemaphoreType.DMA((count,))
    one_sem = pltpu.SemaphoreType.DMA

    evolved = pl.pallas_call(
        evolve_kernel,
        out_shape=jax.ShapeDtypeStruct((N, N, N), F32),
        in_specs=[hbm] * 6,
        out_specs=hbm,
        scratch_shapes=[
            pitched, pitched, pitched, *small, gates, gates, gates, square, square, square,
            pltpu.VMEM((3, 2 * N, 2 * N), BF16), sems(5), sems(N), sems(N),
        ],
        compiler_params=pltpu.CompilerParams(vmem_limit_bytes=VMEM_BYTES),
        name="evolve",
    )(edges, couplings, gates_low, gates_mid, gates_high, initial_state)

    gathered = lax.all_to_all(evolved, AXES, 0, 0, tiled=True)

    mixed = pl.pallas_call(
        mix_kernel,
        out_shape=jax.ShapeDtypeStruct((N, PITCH, N), F32),
        in_specs=[hbm] * 4,
        out_specs=hbm,
        scratch_shapes=[
            cube, cube, pltpu.VMEM((N, 8, N), F32), *small, square, square, square, square,
            pltpu.VMEM((2 * N, 2 * N), BF16), sems(3), sems(N), sems(N), one_sem,
        ],
        compiler_params=pltpu.CompilerParams(vmem_limit_bytes=VMEM_BYTES),
        name="mix",
    )(edges, couplings, top_gate, gathered)

    returned = lax.all_to_all(mixed, AXES, 0, 0, tiled=True)

    return pl.pallas_call(
        finish_kernel,
        out_shape=jax.ShapeDtypeStruct(initial_state.shape, F32),
        in_specs=[hbm],
        out_specs=hbm,
        scratch_shapes=[cube, pltpu.VMEM((N, 8, N), F32), one_sem, sems(N // PIECE), sems(N)],
        compiler_params=pltpu.CompilerParams(vmem_limit_bytes=VMEM_BYTES),
        name="finish",
    )(returned)


def solution(mesh):
    in_specs = (P(AXES, None), P(), P(), P(), P(), P(), P())
    return jax.shard_map(local, mesh=mesh, in_specs=in_specs, out_specs=P(AXES, None), check_vma=False)
```

```python
import jax
import jax.numpy as jnp
from jax import lax
from jax.experimental import pallas as pl
from jax.experimental.pallas import tpu as pltpu
from jax.sharding import PartitionSpec as P

HIGHEST = lax.Precision.HIGHEST
F32 = jnp.float32
BF16 = jnp.bfloat16
N = 128
BITS = 7
LAYERS = 6
AXES = ("gx", "gy")
GROUP = 32
PITCH = N + 8
MIX_GROUP = 32


def mm(a, b):
    return lax.dot_general(a, b, (((1,), (0,)), ((), ())), preferred_element_type=F32)


def mm_nt_exact(a, b):
    return lax.dot_general(
        a, b, (((1,), (1,)), ((), ())), precision=HIGHEST, preferred_element_type=F32
    )


def iota(axis):
    return lax.broadcasted_iota(jnp.int32, (N, N), axis)


def split(x):
    high = x.astype(BF16)
    low = (x - high.astype(F32)).astype(BF16)
    return high, low


def left_pack(gate):
    high, low = split(gate)
    return jnp.concatenate(
        [jnp.concatenate([high, high], axis=1), jnp.concatenate([low, low], axis=1)], axis=0
    )


def right_pack(gate):
    high, low = split(gate.T)
    row = jnp.concatenate([high, low], axis=1)
    return jnp.concatenate([row, row], axis=0)


def left_gate(pack, tiles):
    out = []
    for i in range(0, len(tiles), 2):
        high, low = split(jnp.concatenate(tiles[i : i + 2], axis=1))
        both = mm(pack, jnp.concatenate([high, low], axis=0))
        both = both[:N] + both[N:]
        out += [both[:, :N], both[:, N:]]
    return out


def right_gate(pack, tiles):
    out = []
    for i in range(0, len(tiles), 2):
        high, low = split(jnp.concatenate(tiles[i : i + 2], axis=0))
        both = mm(jnp.concatenate([high, low], axis=1), pack)
        both = both[:, :N] + both[:, N:]
        out += [both[:N], both[N:]]
    return out


def spins(start, value):
    qubit = iota(1)
    inside = (qubit >= start) & (qubit < start + BITS)
    shift = jnp.clip(start + BITS - 1 - qubit, 0, BITS - 1)
    bit = jnp.right_shift(value, shift) & 1
    return jnp.where(inside, 1 - 2 * bit, 0).astype(F32)


def coupling_matrix(edge_ref, coupling_ref):
    names = lax.broadcasted_iota(jnp.int32, (N, edge_ref.shape[1]), 0)
    first = (edge_ref[0:1, :] == names).astype(F32) * coupling_ref[...]
    second = (edge_ref[1:2, :] == names).astype(F32)
    one_way = mm_nt_exact(first, second)
    return one_way + one_way.T


def flat_position():
    return lax.axis_index("gx") * lax.axis_size("gy") + lax.axis_index("gy")


def pieces_of(x):
    first = x.astype(BF16)
    rest = x - first.astype(F32)
    second = rest.astype(BF16)
    return [first, second, (rest - second.astype(F32)).astype(BF16)]


def spin_form(fields, spin_sets):
    left = jnp.concatenate([part for field in fields for part in pieces_of(field)], axis=1)
    right = jnp.concatenate([spin_set.astype(BF16) for spin_set in spin_sets for _ in range(3)], axis=1)
    return lax.dot_general(left, right, (((1,), (1,)), ((), ())), preferred_element_type=F32)


def pair_factors(matrix, fixed, rows, planes, lanes):
    every = jnp.concatenate([rows, planes, lanes, fixed], axis=0).astype(BF16)
    fields = mm(every, jnp.concatenate(pieces_of(matrix), axis=1))
    fields = fields[:, :N] + fields[:, N : 2 * N] + fields[:, 2 * N :]
    row_field, plane_field, lane_field, fixed_field = (fields[i * N : (i + 1) * N] for i in range(4))
    row_energy = jnp.sum((0.5 * row_field + fixed_field) * rows + 0.5 * fixed_field * fixed, axis=1, keepdims=True)
    plane_energy = jnp.sum((0.5 * plane_field + fixed_field) * planes, axis=1, keepdims=True)
    lane_energy = jnp.sum((0.5 * lane_field + fixed_field) * lanes, axis=1, keepdims=True)
    across = jnp.broadcast_to(lane_energy, (N, N)).T
    over_lanes = jnp.exp(spin_form([row_field], [lanes]) + row_energy)
    over_rows = jnp.exp(spin_form([row_field], [planes]))
    over_planes = jnp.exp(spin_form([plane_field], [lanes]) + (plane_energy + across))
    return over_lanes, over_rows, over_planes


def plane_tile(plane):
    return pl.ds(pl.multiple_of(plane * PITCH, 8), N)


def row_tile(row):
    return pl.ds(row, N, stride=PITCH)


def each(count, body):
    def step(i, c):
        body(i)
        return c

    lax.fori_loop(0, count, step, 0)


def sweep(body):
    each(N // GROUP, lambda i: body(i * GROUP))


def start_copies(sem, *pairs):
    copies = [pltpu.make_async_copy(source, target, sem.at[i]) for i, (source, target) in enumerate(pairs)]
    for copy in copies:
        copy.start()
    return copies


def evolve_kernel(edge_hbm, coupling_hbm, low_hbm, mid_hbm, high_hbm, top_hbm, state_ref,
                  out_ref, mix_factors_ref, mix_packs_ref,
                  landed, by_plane, by_row, factor, row_factor, edge_ref, coupling_ref, low_ref, mid_ref, high_ref, top_ref,
                  lane_part, plane_part, turning, packs, small_sem, in_sem, out_sem):
    def load(group):
        columns = pl.ds(pl.multiple_of(group * GROUP * N, GROUP * N), GROUP * N)
        return pltpu.make_async_copy(state_ref.at[:, columns], landed.at[:, columns], in_sem.at[group])

    def store(row):
        return pltpu.make_async_copy(by_row.at[plane_tile(row)], out_ref.at[:, row], out_sem)

    small = start_copies(
        small_sem,
        (edge_hbm, edge_ref), (coupling_hbm, coupling_ref),
        (high_hbm, high_ref), (low_hbm, low_ref), (mid_hbm, mid_ref), (top_hbm, top_ref),
    )
    each(N // GROUP, lambda group: load(group).start())
    for copy in small[:2]:
        copy.wait()
    matrix = coupling_matrix(edge_ref, coupling_ref)
    lane_part[...], turning[...], plane_part[...] = pair_factors(
        matrix,
        spins(0, flat_position()),
        spins(BITS, iota(0)),
        spins(2 * BITS, iota(0)),
        spins(3 * BITS, iota(0)),
    )
    for copy in small[2:]:
        copy.wait()
    packs[0] = left_pack(high_ref[0])
    packs[1] = right_pack(low_ref[0])

    def first(plane):
        load(plane // GROUP).wait()
        columns = turning[...]
        tiles = []
        for j in range(GROUP):
            scale = lane_part[...] * (plane_part[pl.ds(plane + j, 1), :] * columns[:, j : j + 1])
            factor[plane_tile(plane + j)] = scale
            tiles.append(landed[:, pl.ds(pl.multiple_of((plane + j) * N, N), N)] * scale)
        turning[...] = pltpu.roll(columns, N - GROUP, 1)
        tiles = right_gate(packs[1], left_gate(packs[0], tiles))
        for j in range(GROUP):
            by_plane[plane_tile(plane + j)] = tiles[j]

    sweep(first)

    for layer in range(1, LAYERS):
        rows_now = layer % 2 == 1
        across = mid_ref if rows_now else high_ref
        packs[0] = left_pack(across[layer - 1])
        packs[1] = left_pack(across[layer])
        packs[2] = right_pack(low_ref[layer])
        source, target = (by_plane, by_row) if rows_now else (by_row, by_plane)

        def middle(index, layer=layer, rows_now=rows_now, source=source, target=target):
            tiles = left_gate(packs[0], [source[row_tile(index + j)] for j in range(GROUP)])
            for j in range(GROUP):
                if rows_now and layer > 1:
                    scale = row_factor[plane_tile(index + j)]
                elif rows_now:
                    scale = factor[row_tile(index + j)]
                    row_factor[plane_tile(index + j)] = scale
                else:
                    scale = factor[plane_tile(index + j)]
                tiles[j] = tiles[j] * scale
            tiles = right_gate(packs[2], left_gate(packs[1], tiles))
            for j in range(GROUP):
                target[plane_tile(index + j)] = tiles[j]
            if layer == LAYERS - 1:
                each(GROUP, lambda j: store(index + j).start())

        sweep(middle)

    mix_packs_ref[0] = left_pack(top_ref[...])
    mix_packs_ref[1] = left_pack(high_ref[LAYERS - 1])
    mix_factors_ref[0], mix_factors_ref[1], mix_factors_ref[2] = pair_factors(
        coupling_matrix(edge_ref, coupling_ref),
        spins(2 * BITS, flat_position()),
        spins(BITS, iota(0)),
        spins(0, iota(0)),
        spins(3 * BITS, iota(0)),
    )
    pltpu.make_async_copy(landed, landed, out_sem).wait()


def mix_kernel(factors_ref, packs_ref, in_ref, out_ref, turned, turning):
    turning[...] = factors_ref[1]

    def top(i):
        tiles = []
        for j in range(0, MIX_GROUP, 8):
            rows = pl.ds(pl.multiple_of(i * MIX_GROUP + j, 8), 8)
            block = jnp.swapaxes(in_ref[:, rows, :].reshape(N // 8, 8, 8, N), 1, 2)
            tiles += [block[:, k].reshape(N, N) for k in range(8)]
        tiles = left_gate(packs_ref[0], tiles)
        for j in range(MIX_GROUP):
            turned[plane_tile(i * MIX_GROUP + j)] = tiles[j]

    each(N // MIX_GROUP, top)

    def high(i, total):
        device = i * GROUP
        columns = turning[...]
        tiles = left_gate(packs_ref[1], [turned[row_tile(device + j)] for j in range(GROUP)])
        for j in range(GROUP):
            scale = factors_ref[0] * (factors_ref[2, pl.ds(device + j, 1), :] * columns[:, j : j + 1])
            final = tiles[j] * scale
            out_ref[device + j, :N, :] = final
            total += jnp.sum((final * final).reshape(N // 8, 8, N), axis=0)
        turning[...] = pltpu.roll(columns, N - GROUP, 1)
        return total

    total = lax.fori_loop(0, N // GROUP, high, jnp.zeros((8, N), F32))
    out_ref[:, N:, :] = jnp.broadcast_to(total[None], (N, PITCH - N, N))


def finish_kernel(in_ref, out_ref, held, out_sem):
    def store(block):
        rows = pl.ds(pl.multiple_of(block * 8, 8), 8)
        return pltpu.make_async_copy(held.at[rows], out_ref.at[rows], out_sem.at[block])

    total = lax.fori_loop(0, N, lambda m, c: c + in_ref[m, pl.ds(N, 8), :], jnp.zeros((8, N), F32), unroll=8)
    mean_square = jnp.sum(total) / jnp.float32(N * N * N * N)
    scale = lax.rsqrt(jnp.full((8, N), mean_square + 1e-06, F32))

    def rows_step(block):
        rows = pl.ds(pl.multiple_of(block * 8, 8), 8)
        for m in range(N):
            held[rows, m * N : (m + 1) * N] = in_ref[m, rows, :] * scale
        store(block).start()

    each(N // 8, rows_step)
    each(N // 8, lambda block: store(block).wait())


def local(initial_state, edge_list, couplings, gates_low, gates_mid, gates_high, top_gate):
    edges = edge_list.T
    couplings = couplings.reshape(1, -1)
    vmem = pl.BlockSpec(memory_space=pltpu.VMEM)
    hbm = pl.BlockSpec(memory_space=pltpu.HBM)
    square = pltpu.VMEM((N, N), F32)
    pitched = pltpu.VMEM((N * PITCH, N), F32)
    flat = pltpu.VMEM((N, N * N), F32)
    one_sem = pltpu.SemaphoreType.DMA
    gates = pltpu.VMEM((LAYERS, N, N), F32)
    small = [pltpu.VMEM(edges.shape, jnp.int32), pltpu.VMEM(couplings.shape, F32)]
    sems = lambda count: pltpu.SemaphoreType.DMA((count,))

    evolved, mix_factors, mix_packs = pl.pallas_call(
        evolve_kernel,
        out_shape=[
            jax.ShapeDtypeStruct((N, N, N), F32),
            jax.ShapeDtypeStruct((3, N, N), F32),
            jax.ShapeDtypeStruct((2, 2 * N, 2 * N), BF16),
        ],
        in_specs=[hbm] * 7,
        out_specs=[hbm, vmem, vmem],
        scratch_shapes=[
            flat, pitched, pitched, pitched, pitched, *small, gates, gates, gates, square, square, square, square,
            pltpu.VMEM((3, 2 * N, 2 * N), BF16), sems(6), sems(N // GROUP), one_sem,
        ],
        compiler_params=pltpu.CompilerParams(vmem_limit_bytes=60 * 2**20),
        name="evolve",
    )(edges, couplings, gates_low, gates_mid, gates_high, top_gate, initial_state)

    gathered = lax.all_to_all(evolved, AXES, 0, 0, tiled=True)

    mixed = pl.pallas_call(
        mix_kernel,
        out_shape=jax.ShapeDtypeStruct((N, PITCH, N), F32),
        in_specs=[vmem] * 3,
        out_specs=vmem,
        scratch_shapes=[pitched, square],
        compiler_params=pltpu.CompilerParams(vmem_limit_bytes=28 * 2**20),
        name="mix",
    )(mix_factors, mix_packs, gathered)

    returned = lax.all_to_all(mixed, AXES, 0, 0, tiled=True)

    return pl.pallas_call(
        finish_kernel,
        out_shape=jax.ShapeDtypeStruct(initial_state.shape, F32),
        in_specs=[vmem],
        out_specs=hbm,
        scratch_shapes=[flat, sems(N // 8)],
        compiler_params=pltpu.CompilerParams(vmem_limit_bytes=32 * 2**20),
        name="finish",
    )(returned)


def solution(mesh):
    in_specs = (P(AXES, None), P(), P(), P(), P(), P(), P())
    return jax.shard_map(local, mesh=mesh, in_specs=in_specs, out_specs=P(AXES, None), check_vma=False)
```

```python
import jax
import jax.numpy as jnp
from jax import lax
from jax.experimental import pallas as pl
from jax.experimental.pallas import tpu as pltpu
from jax.sharding import PartitionSpec as P

HIGHEST = lax.Precision.HIGHEST
F32 = jnp.float32
BF16 = jnp.bfloat16
N = 128
BITS = 7
LAYERS = 6
AXES = ("gx", "gy")
EXCHANGE = ("gy", "gx")
GROUP = 32
WIDE_GROUP = 64
PITCH = N + 1
BLOCK = N + 8


def mm(a, b):
    return lax.dot_general(a, b, (((1,), (0,)), ((), ())), preferred_element_type=F32)


def mm_nt_exact(a, b):
    return lax.dot_general(
        a, b, (((1,), (1,)), ((), ())), precision=HIGHEST, preferred_element_type=F32
    )


def iota(axis):
    return lax.broadcasted_iota(jnp.int32, (N, N), axis)


def split(x):
    high = x.astype(BF16)
    low = (x - high.astype(F32)).astype(BF16)
    return high, low


def left_pack(gate):
    high, low = split(gate)
    return jnp.concatenate(
        [jnp.concatenate([high, high], axis=1), jnp.concatenate([low, low], axis=1)], axis=0
    )


def right_pack(gate):
    high, low = split(gate.T)
    row = jnp.concatenate([high, low], axis=1)
    return jnp.concatenate([row, row], axis=0)


def left_gate(pack, tiles):
    out = []
    for i in range(0, len(tiles), 2):
        high, low = split(jnp.concatenate(tiles[i : i + 2], axis=1))
        both = mm(pack, jnp.concatenate([high, low], axis=0))
        both = both[:N] + both[N:]
        out += [both[:, :N], both[:, N:]]
    return out


def right_gate(pack, tiles):
    out = []
    for i in range(0, len(tiles), 2):
        high, low = split(jnp.concatenate(tiles[i : i + 2], axis=0))
        both = mm(jnp.concatenate([high, low], axis=1), pack)
        both = both[:, :N] + both[:, N:]
        out += [both[:N], both[N:]]
    return out


def spins(start, value):
    qubit = iota(1)
    inside = (qubit >= start) & (qubit < start + BITS)
    shift = jnp.clip(start + BITS - 1 - qubit, 0, BITS - 1)
    bit = jnp.right_shift(value, shift) & 1
    return jnp.where(inside, 1 - 2 * bit, 0).astype(F32)


def coupling_matrix(edge_ref, coupling_ref):
    names = lax.broadcasted_iota(jnp.int32, (N, edge_ref.shape[1]), 0)
    first = (edge_ref[0:1, :] == names).astype(F32) * coupling_ref[...]
    second = (edge_ref[1:2, :] == names).astype(F32)
    one_way = mm_nt_exact(first, second)
    return one_way + one_way.T


def flat_position(axes):
    return lax.axis_index(axes[0]) * lax.axis_size(axes[1]) + lax.axis_index(axes[1])


def exchange_order(value):
    return lax.rem(value, lax.axis_size("gx")) * lax.axis_size("gy") + lax.div(value, lax.axis_size("gx"))


def pieces_of(x):
    first = x.astype(BF16)
    rest = x - first.astype(F32)
    second = rest.astype(BF16)
    return [first, second, (rest - second.astype(F32)).astype(BF16)]


def spin_form(fields, spin_sets):
    left = jnp.concatenate([part for field in fields for part in pieces_of(field)], axis=1)
    right = jnp.concatenate([spin_set.astype(BF16) for spin_set in spin_sets for _ in range(3)], axis=1)
    return lax.dot_general(left, right, (((1,), (1,)), ((), ())), preferred_element_type=F32)


def pair_factors(matrix, fixed, rows, planes, lanes):
    every = jnp.concatenate([rows, planes, lanes, fixed], axis=0).astype(BF16)
    fields = mm(every, jnp.concatenate(pieces_of(matrix), axis=1))
    fields = fields[:, :N] + fields[:, N : 2 * N] + fields[:, 2 * N :]
    row_field, plane_field, lane_field, fixed_field = (fields[i * N : (i + 1) * N] for i in range(4))
    row_energy = jnp.sum((0.5 * row_field + fixed_field) * rows + 0.5 * fixed_field * fixed, axis=1, keepdims=True)
    plane_energy = jnp.sum((0.5 * plane_field + fixed_field) * planes, axis=1, keepdims=True)
    lane_energy = jnp.sum((0.5 * lane_field + fixed_field) * lanes, axis=1, keepdims=True)
    across = jnp.broadcast_to(lane_energy, (N, N)).T
    over_lanes = jnp.exp(spin_form([row_field], [lanes]) + row_energy)
    over_rows = jnp.exp(spin_form([row_field], [planes]))
    over_planes = jnp.exp(spin_form([plane_field], [lanes]) + (plane_energy + across))
    return over_lanes, over_rows, over_planes


def plane_tile(plane):
    return pl.ds(plane * PITCH, N)


def row_tile(row):
    return pl.ds(row, N, stride=PITCH)


def each(count, body):
    def step(i, c):
        body(i)
        return c

    lax.fori_loop(0, count, step, 0)


def sweep(body, group):
    each(N // group, lambda i: body(i * group))


def reorder(gate):
    to_place = (exchange_order(iota(0)) == iota(1)).astype(BF16)
    rows = sum(mm(to_place, part) for part in pieces_of(gate))
    both = sum(mm(to_place, part) for part in pieces_of(rows.T))
    return both.T


def start_copies(sem, *pairs):
    copies = [pltpu.make_async_copy(source, target, sem.at[i]) for i, (source, target) in enumerate(pairs)]
    for copy in copies:
        copy.start()
    return copies


def evolve_kernel(edge_hbm, coupling_hbm, low_hbm, mid_hbm, high_hbm, top_hbm, state_ref,
                  out_ref, mix_factors_ref, mix_packs_ref,
                  landed, leaving, by_plane, by_row, factor, row_factor, edge_ref, coupling_ref, low_ref, mid_ref, high_ref, top_ref,
                  lane_part, plane_part, turning, packs, small_sem, in_sem, out_sem):
    def load(group):
        columns = pl.ds(pl.multiple_of(group * GROUP * N, GROUP * N), GROUP * N)
        return pltpu.make_async_copy(state_ref.at[:, columns], landed.at[:, columns], in_sem.at[group])

    def store(row):
        return pltpu.make_async_copy(leaving.at[row], out_ref.at[:, row], out_sem)

    load(0).start()
    small = start_copies(
        small_sem,
        (edge_hbm, edge_ref), (coupling_hbm, coupling_ref),
        (high_hbm, high_ref), (low_hbm, low_ref), (mid_hbm, mid_ref), (top_hbm, top_ref),
    )
    each(N // GROUP - 1, lambda group: load(group + 1).start())
    for copy in small[:2]:
        copy.wait()
    matrix = coupling_matrix(edge_ref, coupling_ref)
    lane_part[...], turning[...], plane_part[...] = pair_factors(
        matrix,
        spins(0, flat_position(AXES)),
        spins(BITS, iota(0)),
        spins(2 * BITS, iota(0)),
        spins(3 * BITS, iota(0)),
    )
    for copy in small[2:]:
        copy.wait()
    packs[0] = left_pack(high_ref[0])
    packs[1] = right_pack(low_ref[0])

    def first(plane):
        load(plane // GROUP).wait()
        columns = turning[...]
        tiles = []
        for j in range(GROUP):
            scale = lane_part[...] * (plane_part[pl.ds(plane + j, 1), :] * columns[:, j : j + 1])
            factor[plane_tile(plane + j)] = scale
            tiles.append(landed[:, pl.ds(pl.multiple_of((plane + j) * N, N), N)] * scale)
        turning[...] = pltpu.roll(columns, N - GROUP, 1)
        tiles = right_gate(packs[1], left_gate(packs[0], tiles))
        for j in range(GROUP):
            by_plane[plane_tile(plane + j)] = tiles[j]

    sweep(first, GROUP)

    for layer in range(1, LAYERS):
        rows_now = layer % 2 == 1
        across = mid_ref if rows_now else high_ref
        packs[0] = left_pack(across[layer - 1])
        packs[1] = left_pack(across[layer])
        packs[2] = right_pack(low_ref[layer])
        source, target = (by_plane, by_row) if rows_now else (by_row, by_plane)

        ending = layer == LAYERS - 1
        group = GROUP if ending else WIDE_GROUP

        def middle(index, layer=layer, rows_now=rows_now, source=source, target=target, ending=ending, group=group):
            tiles = left_gate(packs[0], [source[row_tile(index + j)] for j in range(group)])
            for j in range(group):
                if rows_now and layer > 1:
                    scale = row_factor[plane_tile(index + j)]
                elif rows_now:
                    scale = factor[row_tile(index + j)]
                    row_factor[plane_tile(index + j)] = scale
                else:
                    scale = factor[plane_tile(index + j)]
                tiles[j] = tiles[j] * scale
            tiles = right_gate(packs[2], left_gate(packs[1], tiles))
            for j in range(group):
                if ending:
                    leaving[index + j] = tiles[j]
                else:
                    target[plane_tile(index + j)] = tiles[j]
            if ending:
                each(group, lambda j: store(index + j).start())

        sweep(middle, group)

    mix_packs_ref[0] = left_pack(reorder(top_ref[...]))
    mix_packs_ref[1] = left_pack(high_ref[LAYERS - 1])
    mix_factors_ref[0], mix_factors_ref[1], mix_factors_ref[2] = pair_factors(
        coupling_matrix(edge_ref, coupling_ref),
        spins(2 * BITS, flat_position(EXCHANGE)),
        spins(BITS, iota(0)),
        spins(0, exchange_order(iota(0))),
        spins(3 * BITS, iota(0)),
    )
    pltpu.make_async_copy(landed, landed, out_sem).wait()


def mix_kernel(factors_ref, packs_ref, in_ref, out_ref, turned, turning):
    turning[...] = factors_ref[1]

    def top(i):
        tiles = []
        for j in range(0, WIDE_GROUP, 8):
            rows = pl.ds(pl.multiple_of(i * WIDE_GROUP + j, 8), 8)
            block = jnp.swapaxes(in_ref[:, rows, :].reshape(N // 8, 8, 8, N), 1, 2)
            tiles += [block[:, k].reshape(N, N) for k in range(8)]
        tiles = left_gate(packs_ref[0], tiles)
        for j in range(WIDE_GROUP):
            turned[plane_tile(i * WIDE_GROUP + j)] = tiles[j]

    each(N // WIDE_GROUP, top)

    def high(i, total):
        device = i * GROUP
        columns = turning[...]
        tiles = left_gate(packs_ref[1], [turned[row_tile(device + j)] for j in range(GROUP)])
        for j in range(GROUP):
            scale = factors_ref[0] * (factors_ref[2, pl.ds(device + j, 1), :] * columns[:, j : j + 1])
            final = tiles[j] * scale
            out_ref[device + j, :N, :] = final
            total += jnp.sum((final * final).reshape(N // 8, 8, N), axis=0)
        turning[...] = pltpu.roll(columns, N - GROUP, 1)
        return total

    total = lax.fori_loop(0, N // GROUP, high, jnp.zeros((8, N), F32))
    out_ref[:, N:, :] = jnp.broadcast_to(total[None], (N, BLOCK - N, N))


def finish_kernel(in_ref, out_ref, held, out_sem):
    def store(block):
        rows = pl.ds(pl.multiple_of(block * 8, 8), 8)
        return pltpu.make_async_copy(held.at[rows], out_ref.at[rows], out_sem.at[block])

    total = lax.fori_loop(0, N, lambda m, c: c + in_ref[m, pl.ds(N, 8), :], jnp.zeros((8, N), F32), unroll=8)
    mean_square = jnp.sum(total) / jnp.float32(N * N * N * N)
    scale = lax.rsqrt(jnp.full((8, N), mean_square + 1e-06, F32))

    def rows_step(block):
        rows = pl.ds(pl.multiple_of(block * 8, 8), 8)
        for m in range(N):
            held[rows, m * N : (m + 1) * N] = in_ref[m, rows, :] * scale
        store(block).start()

    each(N // 8, rows_step)
    each(N // 8, lambda block: store(block).wait())


def local(initial_state, edge_list, couplings, gates_low, gates_mid, gates_high, top_gate):
    edges = edge_list.T
    couplings = couplings.reshape(1, -1)
    vmem = pl.BlockSpec(memory_space=pltpu.VMEM)
    hbm = pl.BlockSpec(memory_space=pltpu.HBM)
    square = pltpu.VMEM((N, N), F32)
    pitched = pltpu.VMEM((N * PITCH, N), F32)
    flat = pltpu.VMEM((N, N * N), F32)
    one_sem = pltpu.SemaphoreType.DMA
    gates = pltpu.VMEM((LAYERS, N, N), F32)
    small = [pltpu.VMEM(edges.shape, jnp.int32), pltpu.VMEM(couplings.shape, F32)]
    sems = lambda count: pltpu.SemaphoreType.DMA((count,))

    evolved, mix_factors, mix_packs = pl.pallas_call(
        evolve_kernel,
        out_shape=[
            jax.ShapeDtypeStruct((N, N, N), F32),
            jax.ShapeDtypeStruct((3, N, N), F32),
            jax.ShapeDtypeStruct((2, 2 * N, 2 * N), BF16),
        ],
        in_specs=[hbm] * 7,
        out_specs=[hbm, vmem, vmem],
        scratch_shapes=[
            flat, pltpu.VMEM((N, N, N), F32), pitched, pitched, pitched, pitched, *small, gates, gates, gates, square, square, square, square,
            pltpu.VMEM((3, 2 * N, 2 * N), BF16), sems(6), sems(N // GROUP), one_sem,
        ],
        compiler_params=pltpu.CompilerParams(vmem_limit_bytes=60 * 2**20),
        name="evolve",
    )(edges, couplings, gates_low, gates_mid, gates_high, top_gate, initial_state)

    gathered = lax.all_to_all(evolved, EXCHANGE, 0, 0, tiled=True)

    mixed = pl.pallas_call(
        mix_kernel,
        out_shape=jax.ShapeDtypeStruct((N, BLOCK, N), F32),
        in_specs=[vmem] * 3,
        out_specs=vmem,
        scratch_shapes=[pitched, square],
        compiler_params=pltpu.CompilerParams(vmem_limit_bytes=28 * 2**20),
        name="mix",
    )(mix_factors, mix_packs, gathered)

    returned = lax.all_to_all(mixed, EXCHANGE, 0, 0, tiled=True)

    return pl.pallas_call(
        finish_kernel,
        out_shape=jax.ShapeDtypeStruct(initial_state.shape, F32),
        in_specs=[vmem],
        out_specs=hbm,
        scratch_shapes=[flat, sems(N // 8)],
        compiler_params=pltpu.CompilerParams(vmem_limit_bytes=32 * 2**20),
        name="finish",
    )(returned)


def solution(mesh):
    in_specs = (P(AXES, None), P(), P(), P(), P(), P(), P())
    return jax.shard_map(local, mesh=mesh, in_specs=in_specs, out_specs=P(AXES, None), check_vma=False)
```

```python
import jax
import jax.numpy as jnp
from jax import lax
from jax.experimental import pallas as pl
from jax.experimental.pallas import tpu as pltpu
from jax.sharding import PartitionSpec as P

HIGHEST = lax.Precision.HIGHEST
F32 = jnp.float32
BF16 = jnp.bfloat16
N = 128
BITS = 7
LAYERS = 6
AXES = ("gx", "gy")
EXCHANGE = ("gy", "gx")
GROUP = 32
WIDE_GROUP = 64
PITCH = N + 1
BLOCK = N + 8


def mm(a, b):
    return lax.dot_general(a, b, (((1,), (0,)), ((), ())), preferred_element_type=F32)


def mm_nt_exact(a, b):
    return lax.dot_general(
        a, b, (((1,), (1,)), ((), ())), precision=HIGHEST, preferred_element_type=F32
    )


def iota(axis):
    return lax.broadcasted_iota(jnp.int32, (N, N), axis)


def split(x):
    high = x.astype(BF16)
    low = (x - high.astype(F32)).astype(BF16)
    return high, low


def left_pack(gate):
    high, low = split(gate)
    return jnp.concatenate(
        [jnp.concatenate([high, high], axis=1), jnp.concatenate([low, low], axis=1)], axis=0
    )


def right_pack(gate):
    high, low = split(gate.T)
    row = jnp.concatenate([high, low], axis=1)
    return jnp.concatenate([row, row], axis=0)


def left_gate(pack, tiles):
    out = []
    for i in range(0, len(tiles), 2):
        high, low = split(jnp.concatenate(tiles[i : i + 2], axis=1))
        both = mm(pack, jnp.concatenate([high, low], axis=0))
        both = both[:N] + both[N:]
        out += [both[:, :N], both[:, N:]]
    return out


def right_gate(pack, tiles):
    out = []
    for i in range(0, len(tiles), 2):
        high, low = split(jnp.concatenate(tiles[i : i + 2], axis=0))
        both = mm(jnp.concatenate([high, low], axis=1), pack)
        both = both[:, :N] + both[:, N:]
        out += [both[:N], both[N:]]
    return out


def spins(start, value):
    qubit = iota(1)
    inside = (qubit >= start) & (qubit < start + BITS)
    shift = jnp.clip(start + BITS - 1 - qubit, 0, BITS - 1)
    bit = jnp.right_shift(value, shift) & 1
    return jnp.where(inside, 1 - 2 * bit, 0).astype(F32)


def coupling_matrix(edge_ref, coupling_ref):
    names = lax.broadcasted_iota(jnp.int32, (N, edge_ref.shape[1]), 0)
    first = (edge_ref[0:1, :] == names).astype(F32) * coupling_ref[...]
    second = (edge_ref[1:2, :] == names).astype(F32)
    one_way = mm_nt_exact(first, second)
    return one_way + one_way.T


def flat_position(axes):
    return lax.axis_index(axes[0]) * lax.axis_size(axes[1]) + lax.axis_index(axes[1])


def exchange_order(value):
    return lax.rem(value, lax.axis_size("gx")) * lax.axis_size("gy") + lax.div(value, lax.axis_size("gx"))


def pieces_of(x):
    first = x.astype(BF16)
    rest = x - first.astype(F32)
    second = rest.astype(BF16)
    return [first, second, (rest - second.astype(F32)).astype(BF16)]


def spin_form(fields, spin_sets):
    left = jnp.concatenate([part for field in fields for part in pieces_of(field)], axis=1)
    right = jnp.concatenate([spin_set.astype(BF16) for spin_set in spin_sets for _ in range(3)], axis=1)
    return lax.dot_general(left, right, (((1,), (1,)), ((), ())), preferred_element_type=F32)


def pair_factors(matrix, fixed, rows, planes, lanes):
    every = jnp.concatenate([rows, planes, lanes, fixed], axis=0).astype(BF16)
    fields = mm(every, jnp.concatenate(pieces_of(matrix), axis=1))
    fields = fields[:, :N] + fields[:, N : 2 * N] + fields[:, 2 * N :]
    row_field, plane_field, lane_field, fixed_field = (fields[i * N : (i + 1) * N] for i in range(4))
    row_energy = jnp.sum((0.5 * row_field + fixed_field) * rows + 0.5 * fixed_field * fixed, axis=1, keepdims=True)
    plane_energy = jnp.sum((0.5 * plane_field + fixed_field) * planes, axis=1, keepdims=True)
    lane_energy = jnp.sum((0.5 * lane_field + fixed_field) * lanes, axis=1, keepdims=True)
    across = jnp.broadcast_to(lane_energy, (N, N)).T
    over_lanes = jnp.exp(spin_form([row_field], [lanes]) + row_energy)
    over_rows = jnp.exp(spin_form([row_field], [planes]))
    over_planes = jnp.exp(spin_form([plane_field], [lanes]) + (plane_energy + across))
    return over_lanes, over_rows, over_planes


def plane_tile(plane):
    return pl.ds(plane * PITCH, N)


def row_tile(row):
    return pl.ds(row, N, stride=PITCH)


def each(count, body):
    def step(i, c):
        body(i)
        return c

    lax.fori_loop(0, count, step, 0)


def sweep(body, group):
    each(N // group, lambda i: body(i * group))


def reorder(gate):
    to_place = (exchange_order(iota(0)) == iota(1)).astype(BF16)
    rows = sum(mm(to_place, part) for part in pieces_of(gate))
    both = sum(mm(to_place, part) for part in pieces_of(rows.T))
    return both.T


def start_copies(sem, *pairs):
    copies = [pltpu.make_async_copy(source, target, sem.at[i]) for i, (source, target) in enumerate(pairs)]
    for copy in copies:
        copy.start()
    return copies


def evolve_kernel(edge_hbm, coupling_hbm, low_hbm, mid_hbm, high_hbm, top_hbm, state_ref,
                  out_ref, mix_factors_ref, mix_packs_ref,
                  landed, leaving, by_plane, by_row, factor, row_factor, edge_ref, coupling_ref, low_ref, mid_ref, high_ref, top_ref,
                  lane_part, plane_part, turning, packs, small_sem, in_sem, out_sem):
    def load(group):
        columns = pl.ds(pl.multiple_of(group * GROUP * N, GROUP * N), GROUP * N)
        return pltpu.make_async_copy(state_ref.at[:, columns], landed.at[:, columns], in_sem.at[group])

    def store(row):
        return pltpu.make_async_copy(leaving.at[row], out_ref.at[:, row], out_sem)

    load(0).start()
    small = start_copies(
        small_sem,
        (edge_hbm, edge_ref), (coupling_hbm, coupling_ref),
        (high_hbm, high_ref), (low_hbm, low_ref), (mid_hbm, mid_ref), (top_hbm, top_ref),
    )
    each(N // GROUP - 1, lambda group: load(group + 1).start())
    for copy in small[:2]:
        copy.wait()
    matrix = coupling_matrix(edge_ref, coupling_ref)
    lane_part[...], turning[...], plane_part[...] = pair_factors(
        matrix,
        spins(0, flat_position(AXES)),
        spins(BITS, iota(0)),
        spins(2 * BITS, iota(0)),
        spins(3 * BITS, iota(0)),
    )
    for copy in small[2:]:
        copy.wait()
    packs[0, 0] = left_pack(high_ref[0])
    packs[0, 1] = right_pack(low_ref[0])

    def prepare(layer):
        if layer < LAYERS:
            across = mid_ref if layer % 2 == 1 else high_ref
            packs[layer % 2, 0] = left_pack(across[layer - 1])
            packs[layer % 2, 1] = left_pack(across[layer])
            packs[layer % 2, 2] = right_pack(low_ref[layer])

    def first(plane):
        load(plane // GROUP).wait()
        columns = turning[...]
        tiles = []
        for j in range(GROUP):
            scale = lane_part[...] * (plane_part[pl.ds(plane + j, 1), :] * columns[:, j : j + 1])
            factor[plane_tile(plane + j)] = scale
            tiles.append(landed[:, pl.ds(pl.multiple_of((plane + j) * N, N), N)] * scale)
        turning[...] = pltpu.roll(columns, N - GROUP, 1)
        tiles = right_gate(packs[0, 1], left_gate(packs[0, 0], tiles))
        prepare(1)
        for j in range(GROUP):
            by_plane[plane_tile(plane + j)] = tiles[j]

    sweep(first, GROUP)

    for layer in range(1, LAYERS):
        rows_now = layer % 2 == 1
        now = packs.at[layer % 2]
        source, target = (by_plane, by_row) if rows_now else (by_row, by_plane)

        ending = layer == LAYERS - 1
        group = GROUP if ending else WIDE_GROUP

        def middle(index, layer=layer, rows_now=rows_now, source=source, target=target, ending=ending, group=group, now=now):
            tiles = left_gate(now[0], [source[row_tile(index + j)] for j in range(group)])
            for j in range(group):
                if rows_now and layer > 1:
                    scale = row_factor[plane_tile(index + j)]
                elif rows_now:
                    scale = factor[row_tile(index + j)]
                    row_factor[plane_tile(index + j)] = scale
                else:
                    scale = factor[plane_tile(index + j)]
                tiles[j] = tiles[j] * scale
            tiles = right_gate(now[2], left_gate(now[1], tiles))
            prepare(layer + 1)
            for j in range(group):
                if ending:
                    leaving[index + j] = tiles[j]
                    store(index + j).start()
                else:
                    target[plane_tile(index + j)] = tiles[j]

        sweep(middle, group)

    mix_packs_ref[0] = left_pack(reorder(top_ref[...]))
    mix_packs_ref[1] = left_pack(high_ref[LAYERS - 1])
    mix_factors_ref[0], mix_factors_ref[1], mix_factors_ref[2] = pair_factors(
        coupling_matrix(edge_ref, coupling_ref),
        spins(2 * BITS, flat_position(EXCHANGE)),
        spins(BITS, iota(0)),
        spins(0, exchange_order(iota(0))),
        spins(3 * BITS, iota(0)),
    )
    pltpu.make_async_copy(landed, landed, out_sem).wait()


def mix_kernel(factors_ref, packs_ref, in_ref, out_ref, turned, turning):
    turning[...] = factors_ref[1]

    def top(i):
        tiles = []
        for j in range(0, WIDE_GROUP, 8):
            rows = pl.ds(pl.multiple_of(i * WIDE_GROUP + j, 8), 8)
            block = jnp.swapaxes(in_ref[:, rows, :].reshape(N // 8, 8, 8, N), 1, 2)
            tiles += [block[:, k].reshape(N, N) for k in range(8)]
        tiles = left_gate(packs_ref[0], tiles)
        for j in range(WIDE_GROUP):
            turned[plane_tile(i * WIDE_GROUP + j)] = tiles[j]

    each(N // WIDE_GROUP, top)

    def high(i, total):
        device = i * WIDE_GROUP
        columns = turning[...]
        tiles = left_gate(packs_ref[1], [turned[row_tile(device + j)] for j in range(WIDE_GROUP)])
        for j in range(WIDE_GROUP):
            scale = factors_ref[0] * (factors_ref[2, pl.ds(device + j, 1), :] * columns[:, j : j + 1])
            final = tiles[j] * scale
            out_ref[device + j, :N, :] = final
            total += jnp.sum((final * final).reshape(N // 8, 8, N), axis=0)
        turning[...] = pltpu.roll(columns, N - WIDE_GROUP, 1)
        return total

    total = lax.fori_loop(0, N // WIDE_GROUP, high, jnp.zeros((8, N), F32))
    out_ref[:, N:, :] = jnp.broadcast_to(total[None], (N, BLOCK - N, N))


def finish_kernel(in_ref, out_ref, held, out_sem):
    def store(block):
        rows = pl.ds(pl.multiple_of(block * 8, 8), 8)
        return pltpu.make_async_copy(held.at[rows], out_ref.at[rows], out_sem.at[block])

    total = lax.fori_loop(0, N, lambda m, c: c + in_ref[m, pl.ds(N, 8), :], jnp.zeros((8, N), F32), unroll=8)
    mean_square = jnp.sum(total) / jnp.float32(N * N * N * N)
    scale = lax.rsqrt(jnp.full((8, N), mean_square + 1e-06, F32))

    def rows_step(block):
        rows = pl.ds(pl.multiple_of(block * 8, 8), 8)
        for m in range(N):
            held[rows, m * N : (m + 1) * N] = in_ref[m, rows, :] * scale
        store(block).start()

    each(N // 8, rows_step)
    each(N // 8, lambda block: store(block).wait())


def local(initial_state, edge_list, couplings, gates_low, gates_mid, gates_high, top_gate):
    edges = edge_list.T
    couplings = couplings.reshape(1, -1)
    vmem = pl.BlockSpec(memory_space=pltpu.VMEM)
    hbm = pl.BlockSpec(memory_space=pltpu.HBM)
    square = pltpu.VMEM((N, N), F32)
    pitched = pltpu.VMEM((N * PITCH, N), F32)
    flat = pltpu.VMEM((N, N * N), F32)
    one_sem = pltpu.SemaphoreType.DMA
    gates = pltpu.VMEM((LAYERS, N, N), F32)
    small = [pltpu.VMEM(edges.shape, jnp.int32), pltpu.VMEM(couplings.shape, F32)]
    sems = lambda count: pltpu.SemaphoreType.DMA((count,))

    evolved, mix_factors, mix_packs = pl.pallas_call(
        evolve_kernel,
        out_shape=[
            jax.ShapeDtypeStruct((N, N, N), F32),
            jax.ShapeDtypeStruct((3, N, N), F32),
            jax.ShapeDtypeStruct((2, 2 * N, 2 * N), BF16),
        ],
        in_specs=[hbm] * 7,
        out_specs=[hbm, vmem, vmem],
        scratch_shapes=[
            flat, pltpu.VMEM((N, N, N), F32), pitched, pitched, pitched, pitched, *small, gates, gates, gates, square, square, square, square,
            pltpu.VMEM((2, 3, 2 * N, 2 * N), BF16), sems(6), sems(N // GROUP), one_sem,
        ],
        compiler_params=pltpu.CompilerParams(vmem_limit_bytes=60 * 2**20),
        name="evolve",
    )(edges, couplings, gates_low, gates_mid, gates_high, top_gate, initial_state)

    gathered = lax.all_to_all(evolved, EXCHANGE, 0, 0, tiled=True)

    mixed = pl.pallas_call(
        mix_kernel,
        out_shape=jax.ShapeDtypeStruct((N, BLOCK, N), F32),
        in_specs=[vmem] * 3,
        out_specs=vmem,
        scratch_shapes=[pitched, square],
        compiler_params=pltpu.CompilerParams(vmem_limit_bytes=28 * 2**20),
        name="mix",
    )(mix_factors, mix_packs, gathered)

    returned = lax.all_to_all(mixed, EXCHANGE, 0, 0, tiled=True)

    return pl.pallas_call(
        finish_kernel,
        out_shape=jax.ShapeDtypeStruct(initial_state.shape, F32),
        in_specs=[vmem],
        out_specs=hbm,
        scratch_shapes=[flat, sems(N // 8)],
        compiler_params=pltpu.CompilerParams(vmem_limit_bytes=32 * 2**20),
        name="finish",
    )(returned)


def solution(mesh):
    in_specs = (P(AXES, None), P(), P(), P(), P(), P(), P())
    return jax.shard_map(local, mesh=mesh, in_specs=in_specs, out_specs=P(AXES, None), check_vma=False)
```

```python
import jax
import jax.numpy as jnp
from jax import lax
from jax.experimental import pallas as pl
from jax.experimental.pallas import tpu as pltpu
from jax.sharding import PartitionSpec as P

HIGHEST = lax.Precision.HIGHEST
F32 = jnp.float32
BF16 = jnp.bfloat16
N = 128
BITS = 7
LAYERS = 6
AXES = ("gx", "gy")
EXCHANGE = ("gy", "gx")
GROUP = 32
WIDE_GROUP = 64
PITCH = N + 1
BLOCK = N + 8


def mm(a, b):
    return lax.dot_general(a, b, (((1,), (0,)), ((), ())), preferred_element_type=F32)


def mm_nt_exact(a, b):
    return lax.dot_general(
        a, b, (((1,), (1,)), ((), ())), precision=HIGHEST, preferred_element_type=F32
    )


def iota(axis):
    return lax.broadcasted_iota(jnp.int32, (N, N), axis)


def split(x):
    high = x.astype(BF16)
    low = (x - high.astype(F32)).astype(BF16)
    return high, low


def left_pack(gate):
    high, low = split(gate)
    return jnp.concatenate(
        [jnp.concatenate([high, high], axis=1), jnp.concatenate([low, low], axis=1)], axis=0
    )


def right_pack(gate):
    high, low = split(gate.T)
    row = jnp.concatenate([high, low], axis=1)
    return jnp.concatenate([row, row], axis=0)


def left_gate(pack, tiles):
    out = []
    for i in range(0, len(tiles), 2):
        high, low = split(jnp.concatenate(tiles[i : i + 2], axis=1))
        both = mm(pack, jnp.concatenate([high, low], axis=0))
        both = both[:N] + both[N:]
        out += [both[:, :N], both[:, N:]]
    return out


def right_gate(pack, tiles):
    out = []
    for i in range(0, len(tiles), 2):
        high, low = split(jnp.concatenate(tiles[i : i + 2], axis=0))
        both = mm(jnp.concatenate([high, low], axis=1), pack)
        both = both[:, :N] + both[:, N:]
        out += [both[:N], both[N:]]
    return out


def spins(start, value):
    qubit = iota(1)
    inside = (qubit >= start) & (qubit < start + BITS)
    shift = jnp.clip(start + BITS - 1 - qubit, 0, BITS - 1)
    bit = jnp.right_shift(value, shift) & 1
    return jnp.where(inside, 1 - 2 * bit, 0).astype(F32)


def coupling_matrix(edge_ref, coupling_ref):
    names = lax.broadcasted_iota(jnp.int32, (N, edge_ref.shape[1]), 0)
    first = (edge_ref[0:1, :] == names).astype(F32) * coupling_ref[...]
    second = (edge_ref[1:2, :] == names).astype(F32)
    one_way = mm_nt_exact(first, second)
    return one_way + one_way.T


def flat_position(axes):
    return lax.axis_index(axes[0]) * lax.axis_size(axes[1]) + lax.axis_index(axes[1])


def exchange_order(value):
    return lax.rem(value, lax.axis_size("gx")) * lax.axis_size("gy") + lax.div(value, lax.axis_size("gx"))


def pieces_of(x):
    first = x.astype(BF16)
    rest = x - first.astype(F32)
    second = rest.astype(BF16)
    return [first, second, (rest - second.astype(F32)).astype(BF16)]


def spin_form(fields, spin_sets):
    left = jnp.concatenate([part for field in fields for part in pieces_of(field)], axis=1)
    right = jnp.concatenate([spin_set.astype(BF16) for spin_set in spin_sets for _ in range(3)], axis=1)
    return lax.dot_general(left, right, (((1,), (1,)), ((), ())), preferred_element_type=F32)


def pair_factors(matrix, fixed, rows, planes, lanes):
    every = jnp.concatenate([rows, planes, lanes, fixed], axis=0).astype(BF16)
    fields = mm(every, jnp.concatenate(pieces_of(matrix), axis=1))
    fields = fields[:, :N] + fields[:, N : 2 * N] + fields[:, 2 * N :]
    row_field, plane_field, lane_field, fixed_field = (fields[i * N : (i + 1) * N] for i in range(4))
    row_energy = jnp.sum((0.5 * row_field + fixed_field) * rows + 0.5 * fixed_field * fixed, axis=1, keepdims=True)
    plane_energy = jnp.sum((0.5 * plane_field + fixed_field) * planes, axis=1, keepdims=True)
    lane_energy = jnp.sum((0.5 * lane_field + fixed_field) * lanes, axis=1, keepdims=True)
    across = jnp.broadcast_to(lane_energy, (N, N)).T
    over_lanes = jnp.exp(spin_form([row_field], [lanes]) + row_energy)
    over_rows = jnp.exp(spin_form([row_field], [planes]))
    over_planes = jnp.exp(spin_form([plane_field], [lanes]) + (plane_energy + across))
    return over_lanes, over_rows, over_planes


def plane_tile(plane):
    return pl.ds(plane * PITCH, N)


def row_tile(row):
    return pl.ds(row, N, stride=PITCH)


def each(count, body):
    def step(i, c):
        body(i)
        return c

    lax.fori_loop(0, count, step, 0)


def sweep(body, group):
    each(N // group, lambda i: body(i * group))


def reorder(gate):
    to_place = (exchange_order(iota(0)) == iota(1)).astype(BF16)
    rows = sum(mm(to_place, part) for part in pieces_of(gate))
    both = sum(mm(to_place, part) for part in pieces_of(rows.T))
    return both.T


def start_copies(sem, *pairs):
    copies = [pltpu.make_async_copy(source, target, sem.at[i]) for i, (source, target) in enumerate(pairs)]
    for copy in copies:
        copy.start()
    return copies


def evolve_kernel(edge_hbm, coupling_hbm, low_hbm, mid_hbm, high_hbm, top_hbm, state_ref,
                  out_ref, mix_factors_ref, mix_packs_ref,
                  landed, leaving, by_plane, by_row, factor, row_factor, edge_ref, coupling_ref, low_ref, mid_ref, high_ref, top_ref,
                  lane_part, plane_part, turning, packs, small_sem, in_sem, out_sem):
    def load(group):
        columns = pl.ds(pl.multiple_of(group * GROUP * N, GROUP * N), GROUP * N)
        return pltpu.make_async_copy(state_ref.at[:, columns], landed.at[:, columns], in_sem.at[group])

    def store(row):
        return pltpu.make_async_copy(leaving.at[row], out_ref.at[:, row], out_sem)

    load(0).start()
    small = start_copies(
        small_sem,
        (edge_hbm, edge_ref), (coupling_hbm, coupling_ref),
        (high_hbm, high_ref), (low_hbm, low_ref), (mid_hbm, mid_ref), (top_hbm, top_ref),
    )
    each(N // GROUP - 1, lambda group: load(group + 1).start())
    for copy in small[:2]:
        copy.wait()
    matrix = coupling_matrix(edge_ref, coupling_ref)
    lane_part[...], turning[...], plane_part[...] = pair_factors(
        matrix,
        spins(0, flat_position(AXES)),
        spins(BITS, iota(0)),
        spins(2 * BITS, iota(0)),
        spins(3 * BITS, iota(0)),
    )
    for copy in small[2:]:
        copy.wait()
    packs[0, 0] = left_pack(high_ref[0])
    packs[0, 1] = right_pack(low_ref[0])

    def prepare(layer):
        if layer < LAYERS:
            across = mid_ref if layer % 2 == 1 else high_ref
            packs[layer % 2, 0] = left_pack(across[layer - 1])
            packs[layer % 2, 1] = left_pack(across[layer])
            packs[layer % 2, 2] = right_pack(low_ref[layer])

    def first(plane):
        load(plane // GROUP).wait()
        columns = turning[...]
        tiles = []
        for j in range(GROUP):
            scale = lane_part[...] * (plane_part[pl.ds(plane + j, 1), :] * columns[:, j : j + 1])
            factor[plane_tile(plane + j)] = scale
            tiles.append(landed[:, pl.ds(pl.multiple_of((plane + j) * N, N), N)] * scale)
        turning[...] = pltpu.roll(columns, N - GROUP, 1)
        tiles = right_gate(packs[0, 1], left_gate(packs[0, 0], tiles))
        prepare(1)
        for j in range(GROUP):
            by_plane[plane_tile(plane + j)] = tiles[j]

    sweep(first, GROUP)

    for layer in range(1, LAYERS):
        rows_now = layer % 2 == 1
        now = packs.at[layer % 2]
        source, target = (by_plane, by_row) if rows_now else (by_row, by_plane)

        ending = layer == LAYERS - 1
        group = GROUP if ending else WIDE_GROUP

        def middle(index, layer=layer, rows_now=rows_now, source=source, target=target, ending=ending, group=group, now=now):
            tiles = left_gate(now[0], [source[row_tile(index + j)] for j in range(group)])
            for j in range(group):
                if rows_now and layer > 1:
                    scale = row_factor[plane_tile(index + j)]
                elif rows_now:
                    scale = factor[row_tile(index + j)]
                    row_factor[plane_tile(index + j)] = scale
                else:
                    scale = factor[plane_tile(index + j)]
                tiles[j] = tiles[j] * scale
            tiles = right_gate(now[2], left_gate(now[1], tiles))
            prepare(layer + 1)
            for j in range(group):
                if ending:
                    leaving[index + j] = tiles[j]
                    store(index + j).start()
                else:
                    target[plane_tile(index + j)] = tiles[j]

        sweep(middle, group)

    mix_packs_ref[0] = left_pack(reorder(top_ref[...]))
    mix_packs_ref[1] = left_pack(high_ref[LAYERS - 1])
    mix_factors_ref[0], mix_factors_ref[1], mix_factors_ref[2] = pair_factors(
        coupling_matrix(edge_ref, coupling_ref),
        spins(2 * BITS, flat_position(EXCHANGE)),
        spins(BITS, iota(0)),
        spins(0, exchange_order(iota(0))),
        spins(3 * BITS, iota(0)),
    )
    pltpu.make_async_copy(landed, landed, out_sem).wait()


def mix_kernel(factors_ref, packs_ref, in_ref, out_ref, turned, turning):
    turning[...] = factors_ref[1]

    def top(i):
        tiles = []
        for j in range(0, WIDE_GROUP, 8):
            rows = pl.ds(pl.multiple_of(i * WIDE_GROUP + j, 8), 8)
            block = jnp.swapaxes(in_ref[:, rows, :].reshape(N // 8, 8, 8, N), 1, 2)
            tiles += [block[:, k].reshape(N, N) for k in range(8)]
        tiles = left_gate(packs_ref[0], tiles)
        for j in range(WIDE_GROUP):
            turned[plane_tile(i * WIDE_GROUP + j)] = tiles[j]

    each(N // WIDE_GROUP, top)

    def high(i, total):
        device = i * WIDE_GROUP
        columns = turning[...]
        tiles = left_gate(packs_ref[1], [turned[row_tile(device + j)] for j in range(WIDE_GROUP)])
        for j in range(WIDE_GROUP):
            scale = factors_ref[0] * (factors_ref[2, pl.ds(device + j, 1), :] * columns[:, j : j + 1])
            final = tiles[j] * scale
            out_ref[device + j, :N, :] = final
            total += jnp.sum((final * final).reshape(N // 8, 8, N), axis=0)
        turning[...] = pltpu.roll(columns, N - WIDE_GROUP, 1)
        return total

    total = lax.fori_loop(0, N // WIDE_GROUP, high, jnp.zeros((8, N), F32))
    out_ref[:, N:, :] = jnp.broadcast_to(total[None], (N, BLOCK - N, N))


def finish_kernel(in_ref, out_ref, held, out_sem):
    def store(block):
        rows = pl.ds(pl.multiple_of(block * 8, 8), 8)
        return pltpu.make_async_copy(held.at[rows], out_ref.at[rows], out_sem.at[block])

    total = lax.fori_loop(0, N, lambda m, c: c + in_ref[m, pl.ds(N, 8), :], jnp.zeros((8, N), F32), unroll=8)
    mean_square = jnp.sum(total) / jnp.float32(N * N * N * N)
    scale = lax.rsqrt(jnp.full((8, N), mean_square + 1e-06, F32))

    def rows_step(block):
        rows = pl.ds(pl.multiple_of(block * 8, 8), 8)
        for m in range(N):
            held[rows, m * N : (m + 1) * N] = in_ref[m, rows, :] * scale
        store(block).start()

    each(N // 8, rows_step)
    each(N // 8, lambda block: store(block).wait())


def local(initial_state, edge_list, couplings, gates_low, gates_mid, gates_high, top_gate):
    edges = edge_list.T
    couplings = couplings.reshape(1, -1)
    vmem = pl.BlockSpec(memory_space=pltpu.VMEM)
    hbm = pl.BlockSpec(memory_space=pltpu.HBM)
    square = pltpu.VMEM((N, N), F32)
    pitched = pltpu.VMEM((N * (PITCH + 1), N), F32)
    flat = pltpu.VMEM((N, N * N), F32)
    one_sem = pltpu.SemaphoreType.DMA
    gates = pltpu.VMEM((LAYERS, N, N), F32)
    small = [pltpu.VMEM(edges.shape, jnp.int32), pltpu.VMEM(couplings.shape, F32)]
    sems = lambda count: pltpu.SemaphoreType.DMA((count,))

    evolved, mix_factors, mix_packs = pl.pallas_call(
        evolve_kernel,
        out_shape=[
            jax.ShapeDtypeStruct((N, N, N), F32),
            jax.ShapeDtypeStruct((3, N, N), F32),
            jax.ShapeDtypeStruct((2, 2 * N, 2 * N), BF16),
        ],
        in_specs=[hbm] * 7,
        out_specs=[hbm, vmem, vmem],
        scratch_shapes=[
            flat, pltpu.VMEM((N, N, N), F32), pitched, pitched, pitched, pitched, *small, gates, gates, gates, square, square, square, square,
            pltpu.VMEM((2, 3, 2 * N, 2 * N), BF16), sems(6), sems(N // GROUP), one_sem,
        ],
        compiler_params=pltpu.CompilerParams(vmem_limit_bytes=60 * 2**20),
        name="evolve",
    )(edges, couplings, gates_low, gates_mid, gates_high, top_gate, initial_state)

    gathered = lax.all_to_all(evolved, EXCHANGE, 0, 0, tiled=True)

    mixed = pl.pallas_call(
        mix_kernel,
        out_shape=jax.ShapeDtypeStruct((N, BLOCK, N), F32),
        in_specs=[vmem] * 3,
        out_specs=vmem,
        scratch_shapes=[pitched, square],
        compiler_params=pltpu.CompilerParams(vmem_limit_bytes=28 * 2**20),
        name="mix",
    )(mix_factors, mix_packs, gathered)

    returned = lax.all_to_all(mixed, EXCHANGE, 0, 0, tiled=True)

    return pl.pallas_call(
        finish_kernel,
        out_shape=jax.ShapeDtypeStruct(initial_state.shape, F32),
        in_specs=[vmem],
        out_specs=hbm,
        scratch_shapes=[flat, sems(N // 8)],
        compiler_params=pltpu.CompilerParams(vmem_limit_bytes=32 * 2**20),
        name="finish",
    )(returned)


def solution(mesh):
    in_specs = (P(AXES, None), P(), P(), P(), P(), P(), P())
    return jax.shard_map(local, mesh=mesh, in_specs=in_specs, out_specs=P(AXES, None), check_vma=False)
```
